32 devices in a mesh: groups: 2 (over x), replica: 4 (over z), tensor: 4 (over y, core).
Axes of the slice: x: 2, y: 2, z: 4, core: 2. Of those that a mesh axis runs over, the one named last changes fastest.
Arguments:
- hidden_input: bfloat16 [512, 8192], P(('groups', 'replica'), 'tensor'), parts along dimension 0, may hold values from -6 to 6
- norm_gain_vector: float32 [8192], replicated, may hold values from 0.5 to 1.5
- query_weight: bfloat16 [8192, 4096], P(None, 'tensor'), may hold values from -0.0625 to 0.0625
- key_weight: bfloat16 [8192, 512], P(None, 'tensor'), may hold values from -0.0625 to 0.0625
- value_weight: bfloat16 [8192, 512], P(None, 'tensor'), may hold values from -0.0625 to 0.0625
- output_weight: bfloat16 [4096, 8192], P('tensor'), may hold values from -0.09375 to 0.09375
- key_cache_rows: bfloat16 [512, 64, 512], P(('groups', 'replica', 'tensor')), parts along dimension 0, may hold values from -95 to 95
- value_cache_rows: bfloat16 [512, 64, 512], P(('groups', 'replica', 'tensor')), parts along dimension 0, may hold values from -6 to 6
- cache_length: int32 [512], P(('groups', 'replica', 'tensor')), parts along dimension 0, may hold values from 1 to 64, as said below
- adapter_index: int32 [512], P(('groups', 'replica')), parts along dimension 0, may hold values from 0 to 63
- query_down_weight: bfloat16 [128, 8192, 16], P(('groups', 'replica'), 'tensor'), parts along dimension 0, may hold values from -0.0625 to 0.0625
- query_up_weight: bfloat16 [128, 16, 4096], P(('groups', 'replica'), None, 'tensor'), parts along dimension 0, may hold values from -1.5 to 1.5
- output_down_weight: bfloat16 [128, 4096, 16], P(('groups', 'replica'), 'tensor'), parts along dimension 0, may hold values from -0.09375 to 0.09375
- output_up_weight: bfloat16 [128, 16, 8192], P(('groups', 'replica'), None, 'tensor'), parts along dimension 0, may hold values from -1.5 to 1.5
Outputs:
- mixed: bfloat16 [512, 8192], P(('groups', 'replica'), 'tensor'), parts along dimension 0
The draws below stay inside these ranges and needn't reach their ends.
There are 2 independent parts, one for each index of `groups`. The reference program is written for one: setup_inputs(seed, part) draws one part's arguments, and reference() takes and returns one part's arrays. A program takes and returns all parts, laid end to end along the dimension named above; an argument that names none is the same for every part. Nothing has to cross between parts.
Inputs may be any that keep to these rules, and one draw needn't show every extreme that they name: `cache_length`: every request holds at least one live slot; some request holds all 64.
All inputs are finite; a program needn't handle non-finite values.
Results may differ from the reference program's by a relative error of at most 0.0065.
The reference program's roundings to bfloat16 on the way count: a program that leaves them out, or rounds other values in their place, can miss the bound.
Values may be sent and summed in bfloat16 or wider, within the bound.
A program may use at most 128 MiB of HBM per device.

```python
import math
import jax
import jax.numpy as jnp
import numpy as np
from jax import lax

MODEL_WIDTH = 8192
QUERY_HEADS = 32
KV = 4
HEAD_SIZE = 128
ADAPTER_RANK = 16
L = 64
ROW_ATT = 16
ROWS = 256
ADAPTER_TOTAL = 64
N_TENSOR = 4


def draw_cache_length(key, part):
    key = jax.random.fold_in(key, 7)
    first, second = jax.random.split(key)
    spans = jax.random.randint(first, (ROWS,), 1, L + 1)
    chosen = jax.random.randint(second, (), 0, ROWS)
    return jnp.where(jnp.arange(ROWS) == chosen, L, spans).astype(jnp.int32)


def draw_key_cache_rows(key, part):
    key = jax.random.fold_in(key, 11)
    first = jax.random.fold_in(key, 0)
    drawn = jax.random.normal(first, (ROWS, L, KV * HEAD_SIZE), jnp.float32)
    return jnp.clip(drawn, -6.0, 6.0).astype(jnp.bfloat16)


def place_ends(drawn, rng, least, high):
    spot = [jax.random.randint(jax.random.fold_in(rng, axis), (), 0, length) for axis, length in enumerate(drawn.shape)]
    longest = drawn.shape.index(max(drawn.shape))
    beside = spot[:longest] + [(spot[longest] + 1) % drawn.shape[longest]] + spot[longest + 1:]
    return drawn.at[tuple(spot)].set(least).at[tuple(beside)].set(high)


def level_of(rng, extent, pieces, smallest, largest):
    loudness, own = 1.0, jax.random.fold_in(rng, 6)
    for dim, blocks in pieces:
        heights = jnp.exp(jax.random.uniform(jax.random.fold_in(own, dim), (blocks,), jnp.float32, smallest / len(pieces), largest / len(pieces)))
        loudness = loudness * jnp.repeat(heights, extent[dim] // blocks).reshape([-1 if axis == dim else 1 for axis in range(len(extent))])
    return loudness


def rank_bounds(count, lean):
    weights = [(1 << 20) // math.isqrt(standing ** lean) + 1 for standing in range(1, count + 1)]
    deviation = 1 + sum(weights) // (1 << 30)
    return np.cumsum(np.array([max(1, weight // deviation) for weight in weights]))


def skewed_ids(own_key, dims, count, skew):
    table = rank_bounds(count, skew)
    ticket = jax.random.randint(jax.random.fold_in(own_key, 1), dims, 0, int(table[count - 1]))
    standing = jnp.searchsorted(jnp.asarray(table, jnp.int32), ticket, side="right")
    return jax.random.permutation(jax.random.fold_in(own_key, 2), count)[standing].astype(jnp.int32)


def gaussian(own_key, dims, spread, reach, pieces=(), kind=jnp.bfloat16):
    gain = level_of(own_key, dims, pieces, -0.22, 0.18) if pieces else 1.0
    values = jax.random.normal(own_key, dims, jnp.float32) * spread * gain
    return jnp.minimum(jnp.maximum(values, -reach), reach).astype(kind)


def setup_inputs(seed: int = 0, part: int = 0) -> dict:
    seeds = jax.random.split(jax.random.key(seed), 15)
    part_splits = jax.random.split(jax.random.fold_in(seeds[14], part), 15)
    hidden_input = gaussian(part_splits[0], (ROWS, MODEL_WIDTH), 1.0, 6.0, ((0, 4), (1, 4)))
    norm_gain_vector = jnp.clip(1.0 + 0.1 * jax.random.normal(seeds[1], (MODEL_WIDTH,), jnp.float32), 0.5, 1.5)
    query_weight = gaussian(seeds[2], (MODEL_WIDTH, QUERY_HEADS * HEAD_SIZE), MODEL_WIDTH ** -0.5, 0.0625, ((1, 4),))
    key_weight = gaussian(seeds[3], (MODEL_WIDTH, KV * HEAD_SIZE), MODEL_WIDTH ** -0.5, 0.0625, ((1, 4),))
    value_weight = gaussian(seeds[4], (MODEL_WIDTH, KV * HEAD_SIZE), MODEL_WIDTH ** -0.5, 0.0625, ((1, 4),))
    output_weight = gaussian(seeds[5], (QUERY_HEADS * HEAD_SIZE, MODEL_WIDTH), (QUERY_HEADS * HEAD_SIZE) ** -0.5, 0.09375, ((0, 4),))
    key_cache_rows = draw_key_cache_rows(jax.random.fold_in(jax.random.fold_in(seeds[14], part), 71), part)
    value_cache_rows = gaussian(part_splits[7], (ROWS, L, KV * HEAD_SIZE), 1.0, 6.0, ((0, 16),))
    cache_length = draw_cache_length(jax.random.fold_in(jax.random.fold_in(seeds[14], part), 71), part)
    adapter_index = place_ends(skewed_ids(part_splits[9], (ROWS,), ADAPTER_TOTAL, 2), jax.random.fold_in(part_splits[9], 3), 0, ADAPTER_TOTAL - 1).astype(jnp.int32)
    query_down_weight = gaussian(part_splits[10], (ADAPTER_TOTAL, MODEL_WIDTH, ADAPTER_RANK), MODEL_WIDTH ** -0.5, 0.0625, ((0, 4), (1, 4)))
    query_up_weight = gaussian(part_splits[11], (ADAPTER_TOTAL, ADAPTER_RANK, QUERY_HEADS * HEAD_SIZE), ADAPTER_RANK ** -0.5, 1.5, ((0, 4), (2, 4)))
    output_down_weight = gaussian(part_splits[12], (ADAPTER_TOTAL, QUERY_HEADS * HEAD_SIZE, ADAPTER_RANK), (QUERY_HEADS * HEAD_SIZE) ** -0.5, 0.09375, ((0, 4), (1, 4)))
    output_up_weight = gaussian(part_splits[13], (ADAPTER_TOTAL, ADAPTER_RANK, MODEL_WIDTH), ADAPTER_RANK ** -0.5, 1.5, ((0, 4), (2, 4)))
    return {"hidden_input": hidden_input, "norm_gain_vector": norm_gain_vector, "query_weight": query_weight, "key_weight": key_weight, "value_weight": value_weight, "output_weight": output_weight, "key_cache_rows": key_cache_rows, "value_cache_rows": value_cache_rows, "cache_length": cache_length, "adapter_index": adapter_index, "query_down_weight": query_down_weight, "query_up_weight": query_up_weight, "output_down_weight": output_down_weight, "output_up_weight": output_up_weight}


ADAPTER_SCALE = 2.0
ROPE_BASE = 500000.0
EPSILON = 1e-05

def rotate(values, position):
    half = values.shape[-1] // 2
    freq = ROPE_BASE ** (-(jnp.arange(half, dtype=jnp.float32) / half))
    angle = position[:, None, None] * freq[None, None, :]
    first = values[..., :half]
    second = values[..., half:]
    cosine = jnp.cos(angle)
    sine = jnp.sin(angle)
    return jnp.concatenate([first * cosine - second * sine, second * cosine + first * sine], axis=-1)

def attend(query_vectors, key_new, value_new, key_cache_rows, value_cache_rows, cache_length):
    count = query_vectors.shape[0]
    group = QUERY_HEADS // KV
    position = cache_length.astype(jnp.float32)
    rot_query = rotate(query_vectors.astype(jnp.float32).reshape(count, QUERY_HEADS, HEAD_SIZE), position).astype(jnp.bfloat16)
    rotated_key = rotate(key_new.astype(jnp.float32).reshape(count, KV, HEAD_SIZE), position).astype(jnp.bfloat16)
    grouped_query = rot_query.reshape(count, KV, group, HEAD_SIZE).astype(jnp.float32)
    keys = key_cache_rows.reshape(count, L, KV, HEAD_SIZE).astype(jnp.float32)
    values = value_cache_rows.reshape(count, L, KV, HEAD_SIZE).astype(jnp.float32)
    softmax_factor = 1.0 / HEAD_SIZE ** 0.5
    scores = jnp.einsum('bkgd,blkd->bkgl', grouped_query, keys) * softmax_factor
    live = jnp.arange(L)[None, :] < cache_length[:, None]
    scores = jnp.where(live[:, None, None, :], scores, -1e+30)
    own_scores = jnp.einsum('enxs,ens->enx', grouped_query, rotated_key.astype(jnp.float32)) * softmax_factor
    top = jnp.maximum(lax.optimization_barrier(jnp.max(scores, axis=-1)), own_scores)
    weights = jnp.exp(scores - top[..., None])
    weight_new = jnp.exp(own_scores - top)
    total = lax.optimization_barrier(jnp.sum(weights, axis=-1)) + weight_new
    probs = (weights / total[..., None]).astype(jnp.bfloat16)
    prob_new = (weight_new / total).astype(jnp.bfloat16)
    context_vectors = jnp.einsum('bkgl,blkd->bkgd', probs.astype(jnp.float32), values)
    fresh = value_new.reshape(count, KV, 1, HEAD_SIZE).astype(jnp.float32)
    context_vectors = context_vectors + prob_new[..., None].astype(jnp.float32) * fresh
    return context_vectors.astype(jnp.bfloat16).reshape(count, QUERY_HEADS * HEAD_SIZE)

def low_rank_output(act, table, adapter_index):
    block = ROW_ATT * N_TENSOR
    blocks = act.shape[0] // block

    def one_block(pair):
        rows, ids = pair
        return jnp.einsum('rd,rdk->rk', rows.astype(jnp.float32), table[ids].astype(jnp.float32))
    result = lax.map(one_block, (act.reshape(blocks, block, act.shape[1]), adapter_index.reshape(blocks, block)))
    return result.reshape(act.shape[0], table.shape[2])

def reference(hidden_input, norm_gain_vector, query_weight, key_weight, value_weight, output_weight, key_cache_rows, value_cache_rows, cache_length, adapter_index, query_down_weight, query_up_weight, output_down_weight, output_up_weight):
    residual_stream = hidden_input.astype(jnp.float32)
    scale = lax.rsqrt(lax.optimization_barrier(jnp.mean(residual_stream * residual_stream, axis=-1, keepdims=True)) + EPSILON)
    normed_hidden = (residual_stream * scale * norm_gain_vector).astype(jnp.bfloat16)
    query_base = jnp.dot(normed_hidden, query_weight, preferred_element_type=jnp.float32)
    query_low_rank = low_rank_output(normed_hidden, query_down_weight, adapter_index).astype(jnp.bfloat16)
    query_vectors = (query_base + ADAPTER_SCALE * low_rank_output(query_low_rank, query_up_weight, adapter_index)).astype(jnp.bfloat16)
    key_new = jnp.dot(normed_hidden, key_weight, preferred_element_type=jnp.float32).astype(jnp.bfloat16)
    value_new = jnp.dot(normed_hidden, value_weight, preferred_element_type=jnp.float32).astype(jnp.bfloat16)
    context_vectors = attend(query_vectors, key_new, value_new, key_cache_rows, value_cache_rows, cache_length)
    output_low_rank = low_rank_output(context_vectors, output_down_weight, adapter_index).astype(jnp.bfloat16)
    base_projection = jnp.dot(context_vectors, output_weight, preferred_element_type=jnp.float32)
    return (residual_stream + base_projection + ADAPTER_SCALE * low_rank_output(output_low_rank, output_up_weight, adapter_index)).astype(jnp.bfloat16)
```

```python
import jax
import jax.numpy as jnp
from jax import lax
from jax.sharding import PartitionSpec as P

QUERY_HEADS = 32
KV = 4
HEAD_SIZE = 128
L = 64


ADAPTER_SCALE = 2.0
ROPE_BASE = 500000.0
EPSILON = 1e-05


def rotate(values, position):
    half = values.shape[-1] // 2
    freq = ROPE_BASE ** (-(jnp.arange(half, dtype=jnp.float32) / half))
    angle = position[:, None, None] * freq[None, None, :]
    first = values[..., :half]
    second = values[..., half:]
    cosine = jnp.cos(angle)
    sine = jnp.sin(angle)
    return jnp.concatenate(
        [first * cosine - second * sine, second * cosine + first * sine], axis=-1
    )


def attend(query_vectors, key_new, value_new, key_cache_rows, value_cache_rows, cache_length):
    count = query_vectors.shape[0]
    group = QUERY_HEADS // KV
    position = cache_length.astype(jnp.float32)
    rot_query = rotate(
        query_vectors.astype(jnp.float32).reshape(count, QUERY_HEADS, HEAD_SIZE), position
    ).astype(jnp.bfloat16)
    rotated_key = rotate(
        key_new.astype(jnp.float32).reshape(count, KV, HEAD_SIZE), position
    ).astype(jnp.bfloat16)
    grouped_query = rot_query.reshape(count, KV, group, HEAD_SIZE)
    keys = key_cache_rows.reshape(count, L, KV, HEAD_SIZE)
    values = value_cache_rows.reshape(count, L, KV, HEAD_SIZE)
    softmax_factor = 1.0 / HEAD_SIZE**0.5
    scores = (
        jnp.einsum("bkgd,blkd->bkgl", grouped_query, keys, preferred_element_type=jnp.float32)
        * softmax_factor
    )
    live = jnp.arange(L)[None, :] < cache_length[:, None]
    scores = jnp.where(live[:, None, None, :], scores, -1e30)
    own_scores = (
        jnp.einsum("enxs,ens->enx", grouped_query, rotated_key, preferred_element_type=jnp.float32)
        * softmax_factor
    )
    top = jnp.maximum(jnp.max(scores, axis=-1), own_scores)
    weights = jnp.exp(scores - top[..., None])
    weight_new = jnp.exp(own_scores - top)
    total = jnp.sum(weights, axis=-1) + weight_new
    probs = (weights / total[..., None]).astype(jnp.bfloat16)
    prob_new = (weight_new / total).astype(jnp.bfloat16)
    context_vectors = jnp.einsum(
        "bkgl,blkd->bkgd", probs, values, preferred_element_type=jnp.float32
    )
    fresh = value_new.reshape(count, KV, 1, HEAD_SIZE).astype(jnp.float32)
    context_vectors = context_vectors + prob_new[..., None].astype(jnp.float32) * fresh
    return context_vectors.astype(jnp.bfloat16).reshape(count, QUERY_HEADS * HEAD_SIZE)


def local_low(act, table, picked):
    projected = jnp.einsum("rd,adk->rak", act, table, preferred_element_type=jnp.float32)
    return jnp.sum(jnp.where(picked[:, :, None], projected, 0.0), axis=1)


def local_up(low, table, picked):
    count, rank, width = table.shape
    spread = jnp.where(picked[:, :, None], low[:, None, :], jnp.zeros((), jnp.bfloat16))
    return jnp.dot(
        spread.reshape(low.shape[0], count * rank),
        table.reshape(count * rank, width),
        preferred_element_type=jnp.float32,
    )


def adapter_contribution(act, table_down, table_up, picked):
    rows = lax.all_gather(act, "replica", axis=0, tiled=True)
    low = lax.psum(local_low(rows, table_down, picked), "tensor").astype(jnp.bfloat16)
    return lax.psum_scatter(
        local_up(low, table_up, picked), "replica", scatter_dimension=0, tiled=True
    )


def per_device(
    hidden_input,
    norm_gain_vector,
    query_weight,
    key_weight,
    value_weight,
    output_weight,
    key_cache_rows,
    value_cache_rows,
    cache_length,
    adapter_index,
    query_down_weight,
    query_up_weight,
    output_down_weight,
    output_up_weight,
):
    width_local = hidden_input.shape[1]
    every_index = lax.all_gather(adapter_index, "replica", axis=0, tiled=True)
    held = query_down_weight.shape[0]
    mine = lax.axis_index("replica") * held + jnp.arange(held)
    picked = every_index[:, None] == mine[None, :]
    whole = lax.all_gather(hidden_input, "tensor", axis=1, tiled=True)
    residual_stream = whole.astype(jnp.float32)
    scale = lax.rsqrt(jnp.mean(residual_stream * residual_stream, axis=-1, keepdims=True) + EPSILON)
    normed_hidden = (residual_stream * scale * norm_gain_vector).astype(jnp.bfloat16)
    query_base = jnp.dot(normed_hidden, query_weight, preferred_element_type=jnp.float32)
    key_new = jnp.dot(normed_hidden, key_weight, preferred_element_type=jnp.float32).astype(
        jnp.bfloat16
    )
    value_new = jnp.dot(normed_hidden, value_weight, preferred_element_type=jnp.float32).astype(
        jnp.bfloat16
    )
    normed_portion = lax.dynamic_slice_in_dim(
        normed_hidden, lax.axis_index("tensor") * width_local, width_local, 1
    )
    query_vectors = (
        query_base
        + ADAPTER_SCALE
        * adapter_contribution(normed_portion, query_down_weight, query_up_weight, picked)
    ).astype(jnp.bfloat16)
    q_rows, k_rows, v_rows = (
        lax.all_to_all(query_vectors, "tensor", split_axis=0, concat_axis=1, tiled=True),
        lax.all_to_all(key_new, "tensor", split_axis=0, concat_axis=1, tiled=True),
        lax.all_to_all(value_new, "tensor", split_axis=0, concat_axis=1, tiled=True),
    )
    context_vectors = attend(q_rows, k_rows, v_rows, key_cache_rows, value_cache_rows, cache_length)
    context_local = lax.all_to_all(
        context_vectors, "tensor", split_axis=1, concat_axis=0, tiled=True
    )
    base_projection = jnp.dot(context_local, output_weight, preferred_element_type=jnp.float32)
    base_portion = lax.psum_scatter(base_projection, "tensor", scatter_dimension=1, tiled=True)
    extra_output = adapter_contribution(
        context_local, output_down_weight, output_up_weight, picked
    )
    return (hidden_input.astype(jnp.float32) + base_portion + ADAPTER_SCALE * extra_output).astype(
        jnp.bfloat16
    )


def solution(mesh):
    placed = (
        P(("groups", "replica"), "tensor"),
        P(),
        P(None, "tensor"),
        P(None, "tensor"),
        P(None, "tensor"),
        P("tensor", None),
        P(("groups", "replica", "tensor"), None, None),
        P(("groups", "replica", "tensor"), None, None),
        P(("groups", "replica", "tensor")),
        P(("groups", "replica")),
        P(("groups", "replica"), "tensor", None),
        P(("groups", "replica"), None, "tensor"),
        P(("groups", "replica"), "tensor", None),
        P(("groups", "replica"), None, "tensor"),
    )
    return jax.shard_map(
        per_device,
        mesh=mesh,
        in_specs=placed,
        out_specs=P(("groups", "replica"), "tensor"),
        check_vma=False,
    )
```

```python
import functools

import jax
import jax.numpy as jnp
from jax import lax
from jax.experimental import pallas as pl
from jax.experimental.pallas import tpu as pltpu
from jax.sharding import PartitionSpec as P

QUERY_HEADS = 32
KV = 4
HEAD_SIZE = 128
L = 64


ADAPTER_SCALE = 2.0
ROPE_BASE = 500000.0
EPSILON = 1e-05


def rotate(values, position):
    half = values.shape[-1] // 2
    freq = ROPE_BASE ** (-(jnp.arange(half, dtype=jnp.float32) / half))
    angle = position[:, None, None] * freq[None, None, :]
    first = values[..., :half]
    second = values[..., half:]
    cosine = jnp.cos(angle)
    sine = jnp.sin(angle)
    return jnp.concatenate(
        [first * cosine - second * sine, second * cosine + first * sine], axis=-1
    )


def attend(query_vectors, key_new, value_new, key_cache_rows, value_cache_rows, cache_length):
    count = query_vectors.shape[0]
    group = QUERY_HEADS // KV
    position = cache_length.astype(jnp.float32)
    rot_query = rotate(
        query_vectors.astype(jnp.float32).reshape(count, QUERY_HEADS, HEAD_SIZE), position
    ).astype(jnp.bfloat16)
    rotated_key = rotate(
        key_new.astype(jnp.float32).reshape(count, KV, HEAD_SIZE), position
    ).astype(jnp.bfloat16)
    grouped_query = rot_query.reshape(count, KV, group, HEAD_SIZE)
    keys = key_cache_rows.reshape(count, L, KV, HEAD_SIZE)
    values = value_cache_rows.reshape(count, L, KV, HEAD_SIZE)
    softmax_factor = 1.0 / HEAD_SIZE**0.5
    scores = (
        jnp.einsum("bkgd,blkd->bkgl", grouped_query, keys, preferred_element_type=jnp.float32)
        * softmax_factor
    )
    live = jnp.arange(L)[None, :] < cache_length[:, None]
    scores = jnp.where(live[:, None, None, :], scores, -1e30)
    own_scores = (
        jnp.einsum("enxs,ens->enx", grouped_query, rotated_key, preferred_element_type=jnp.float32)
        * softmax_factor
    )
    top = jnp.maximum(jnp.max(scores, axis=-1), own_scores)
    weights = jnp.exp(scores - top[..., None])
    weight_new = jnp.exp(own_scores - top)
    total = jnp.sum(weights, axis=-1) + weight_new
    probs = (weights / total[..., None]).astype(jnp.bfloat16)
    prob_new = (weight_new / total).astype(jnp.bfloat16)
    context_vectors = jnp.einsum(
        "bkgl,blkd->bkgd", probs, values, preferred_element_type=jnp.float32
    )
    fresh = value_new.reshape(count, KV, 1, HEAD_SIZE).astype(jnp.float32)
    context_vectors = context_vectors + prob_new[..., None].astype(jnp.float32) * fresh
    return context_vectors.astype(jnp.bfloat16).reshape(count, QUERY_HEADS * HEAD_SIZE)


MESH = pl.DeviceIdType.MESH
F32 = jnp.float32
BF16 = jnp.bfloat16


def place():
    group, rep, ten = (lax.axis_index(name) for name in ("groups", "replica", "tensor"))

    def peer_r(step, count):
        other = lax.rem(rep + step, count)
        return other, (group, other, ten)

    def peer_t(step, count):
        other = lax.rem(ten + step, count)
        return other, (group, rep, other)

    return rep, ten, peer_r, peer_t


def meet(n_r, n_t, peer_r, peer_t):
    barrier = pltpu.get_barrier_semaphore()
    for step in range(1, n_t):
        pl.semaphore_signal(barrier, inc=1, device_id=peer_t(step, n_t)[1], device_id_type=MESH)
    for step in range(1, n_r):
        pl.semaphore_signal(barrier, inc=1, device_id=peer_r(step, n_r)[1], device_id_type=MESH)
    pl.semaphore_wait(barrier, n_t + n_r - 2)


def remote(src, dst, sems, step, device):
    copy = pltpu.make_async_remote_copy(
        src_ref=src,
        dst_ref=dst,
        send_sem=sems.at[0, step],
        recv_sem=sems.at[1, step],
        device_id=device,
        device_id_type=MESH,
    )
    copy.start()
    return copy


def held_mask(ids, rep, held, rank):
    shape = (held, rank, ids.shape[1])
    owner = lax.broadcasted_iota(jnp.int32, shape, 0) + rep * held
    return jnp.broadcast_to(ids[0:1, :][None], shape) == owner


def low_of(down, rows, ids, rep, held, rank):
    projected = lax.dot_general(down, rows, (((1,), (1,)), ((), ())), preferred_element_type=F32)
    projected = projected.reshape(held, rank, rows.shape[0])
    return jnp.sum(jnp.where(held_mask(ids, rep, held, rank), projected, 0.0), axis=0)


def up_of(low, up, ids, rep, held, rank):
    low = low.astype(BF16).astype(F32)
    shape = (held, rank, ids.shape[1])
    spread = jnp.where(held_mask(ids, rep, held, rank), jnp.broadcast_to(low[None], shape), 0.0)
    spread = spread.reshape(held * rank, ids.shape[1]).T.astype(BF16)
    return jnp.dot(spread, up, preferred_element_type=F32)


def query_kernel(
    n_r, n_t, held, rank,
    hid, gain, ids, down, up, qw_hbm, kw_hbm, vw_hbm,
    q_out, kv_out, ids_out,
    qw, kw, vw, hid_t, hid_z, ids_z, scale_z, nrm, qbase, qbuf, qin, kvbuf, kvin,
    low_own, low_in, con, con_in,
    wsem, s_hid_t, s_hid_z, s_ids, s_scale, s_kv, s_low, s_con, s_q,
):
    rep, ten, peer_r, peer_t = place()
    rows, width = hid.shape
    loads = [
        pltpu.make_async_copy(src, dst, wsem.at[i])
        for i, (src, dst) in enumerate(((kw_hbm, kw), (vw_hbm, vw), (qw_hbm, qw)))
    ]
    for load in loads:
        load.start()
    meet(n_r, n_t, peer_r, peer_t)
    sent = []
    for step in reversed(range(1, n_t)):
        sent.append(remote(hid, hid_t.at[ten], s_hid_t, step, peer_t(step, n_t)[1]))
    for step in range(1, n_r):
        sent.append(remote(ids, ids_z.at[rep], s_ids, step, peer_r(step, n_r)[1]))
    hidden_z = []
    for step in range(1, n_r):
        hidden_z.append(remote(hid, hid_z.at[rep], s_hid_z, step, peer_r(step, n_r)[1]))
    hid_t[ten] = hid[...]
    ids_z[rep] = ids[...]
    for copy in sent:
        copy.wait()
    total = jnp.zeros((rows, 1), F32)
    for t in range(n_t):
        piece = hid_t[t].astype(F32)
        total = total + jnp.sum(piece * piece, axis=-1, keepdims=True)
    scale = lax.rsqrt(total * (1.0 / (n_t * width)) + EPSILON)
    scale_z[rep] = jnp.broadcast_to(scale, (rows, 128))
    scales = []
    for step in range(1, n_r):
        scales.append(
            remote(scale_z.at[rep], scale_z.at[rep], s_scale, step, peer_r(step, n_r)[1])
        )
    for t in range(n_t):
        nrm[t] = (hid_t[t].astype(F32) * scale * gain[t]).astype(BF16)
    low_own[rep] = low_of(down[...], nrm[ten], ids_z[rep], rep, held, rank)

    def project(weight, t):
        part = weight[pl.ds(pl.multiple_of(t * width, width), width), :]
        return jnp.dot(nrm[t], part, preferred_element_type=F32)

    per = rows // n_t
    for which, (load, weight) in enumerate(((loads[0], kw), (loads[1], vw))):
        load.wait()
        acc = project(weight, 0)
        for t in range(1, n_t):
            acc = acc + project(weight, t)
        kvbuf[:, which] = acc.astype(BF16).reshape(n_t, per, weight.shape[1])
    kvs = []
    for step in range(1, n_t):
        other, device = peer_t(step, n_t)
        kvs.append(remote(kvbuf.at[other], kvin.at[ten], s_kv, step, device))
    kvin[ten] = kvbuf[ten]
    loads[2].wait()
    qbase[...] = project(qw, 0)

    @pl.loop(1, n_t)
    def _(t):
        qbase[...] += project(qw, t)

    for step in range(1, n_r):
        hidden_z[step - 1].wait()
        scales[step - 1].wait()
        source = lax.rem(rep - step + n_r, n_r)
        portion = (hid_z[source].astype(F32) * scale_z[source][:, 0:1] * gain[ten]).astype(BF16)
        low_own[source] = low_of(down[...], portion, ids_z[source], rep, held, rank)
    lows = []
    for step in range(1, n_t):
        lows.append(remote(low_own, low_in.at[ten], s_low, step, peer_t(step, n_t)[1]))
    low_in[ten] = low_own[...]
    for copy in lows:
        copy.wait()
    cons = []
    for step in list(range(1, n_r)) + [0]:
        other, device = peer_r(step, n_r)
        low = low_in[0, other]
        for t in range(1, n_t):
            low = low + low_in[t, other]
        con[other] = up_of(low, up[...], ids_z[other], rep, held, rank)
        if step:
            cons.append(remote(con.at[other], con_in.at[rep], s_con, step, device))
    con_in[rep] = con[rep]
    for copy in cons:
        copy.wait()
    extra = con_in[0]
    for j in range(1, n_r):
        extra = extra + con_in[j]
    query = (qbase[...] + ADAPTER_SCALE * extra).astype(BF16)
    qbuf[...] = query.reshape(qbuf.shape)
    qs = []
    for step in range(1, n_t):
        other, device = peer_t(step, n_t)
        qs.append(remote(qbuf.at[other], qin.at[ten], s_q, step, device))
    qin[ten] = qbuf[ten]
    ids_out[...] = ids_z[...]
    for copy in kvs:
        copy.wait()
    kv_out[...] = kvin[...]
    for copy in qs:
        copy.wait()
    q_out[...] = qin[...]


def output_kernel(
    n_r, n_t, held, rank,
    ctx, hid, ids_z, down, up, ow_hbm,
    out,
    ow, ctx_t, ctx_z, base, base_in, low_own, low_in, con, con_in,
    wsem, s_ctx_t, s_ctx_z, s_base, s_low, s_con,
):
    rep, ten, peer_r, peer_t = place()
    rows, width = hid.shape
    load = pltpu.make_async_copy(ow_hbm, ow, wsem.at[0])
    load.start()
    meet(n_r, n_t, peer_r, peer_t)
    sent = []
    for step in range(1, n_t):
        other, device = peer_t(step, n_t)
        sent.append(remote(ctx.at[other], ctx_t.at[ten], s_ctx_t, step, device))
    ctx_t[ten] = ctx[ten]
    for copy in sent:
        copy.wait()
    local = ctx_t[...].reshape(rows, ctx.shape[2])
    ctx_z[rep] = local
    zs = []
    for step in range(1, n_r):
        zs.append(remote(ctx_z.at[rep], ctx_z.at[rep], s_ctx_z, step, peer_r(step, n_r)[1]))
    low_own[rep] = low_of(down[...], local, ids_z[rep], rep, held, rank)
    load.wait()
    bases = []
    for step in list(range(1, n_t)) + [0]:
        other, device = peer_t(step, n_t)
        columns = pl.ds(pl.multiple_of(other * width, width), width)
        base[other] = jnp.dot(ctx_z[rep], ow[:, columns], preferred_element_type=F32)
        if step:
            bases.append(remote(base.at[other], base_in.at[ten], s_base, step, device))
    base_in[ten] = base[ten]
    for step in range(1, n_r):
        zs[step - 1].wait()
        source = lax.rem(rep - step + n_r, n_r)
        low_own[source] = low_of(down[...], ctx_z[source], ids_z[source], rep, held, rank)
    lows = []
    for step in range(1, n_t):
        lows.append(remote(low_own, low_in.at[ten], s_low, step, peer_t(step, n_t)[1]))
    low_in[ten] = low_own[...]
    for copy in lows:
        copy.wait()
    cons = []
    for step in list(range(1, n_r)) + [0]:
        other, device = peer_r(step, n_r)
        low = low_in[0, other]
        for t in range(1, n_t):
            low = low + low_in[t, other]
        con[other] = up_of(low, up[...], ids_z[other], rep, held, rank)
        if step:
            cons.append(remote(con.at[other], con_in.at[rep], s_con, step, device))
    con_in[rep] = con[rep]
    for copy in bases:
        copy.wait()
    total = base_in[0]
    for t in range(1, n_t):
        total = total + base_in[t]
    total = hid[...].astype(F32) + total
    for copy in cons:
        copy.wait()
    extra = con_in[0]
    for j in range(1, n_r):
        extra = extra + con_in[j]
    out[...] = (total + ADAPTER_SCALE * extra).astype(BF16)


VM = pl.BlockSpec(memory_space=pltpu.VMEM)
ANY = pl.BlockSpec(memory_space=pl.ANY)
LIMIT = 54 * 1024 * 1024


def sems(count):
    return pltpu.SemaphoreType.DMA((2, count))


def per_device(
    n_r,
    n_t,
    hidden_input,
    norm_gain_vector,
    query_weight,
    key_weight,
    value_weight,
    output_weight,
    key_cache_rows,
    value_cache_rows,
    cache_length,
    adapter_index,
    query_down_weight,
    query_up_weight,
    output_down_weight,
    output_up_weight,
):
    rows, width = hidden_input.shape
    held, _, rank = query_down_weight.shape
    per = rows // n_t
    q_w, k_w, o_w = query_weight.shape[1], key_weight.shape[1], output_weight.shape[0]

    def flat_down(table):
        return table.transpose(0, 2, 1).reshape(held * rank, table.shape[1])

    def flat_up(table):
        return table.reshape(held * rank, table.shape[2])

    ids = jnp.broadcast_to(adapter_index[None, :], (8, rows))
    q_in, kv_in, ids_z = pl.pallas_call(
        functools.partial(query_kernel, n_r, n_t, held, rank),
        out_shape=(
            jax.ShapeDtypeStruct((n_t, per, q_w), BF16),
            jax.ShapeDtypeStruct((n_t, 2, per, k_w), BF16),
            jax.ShapeDtypeStruct((n_r, 8, rows), jnp.int32),
        ),
        in_specs=[VM] * 5 + [ANY] * 3,
        out_specs=(VM, VM, VM),
        scratch_shapes=[
            pltpu.VMEM(query_weight.shape, BF16),
            pltpu.VMEM(key_weight.shape, BF16),
            pltpu.VMEM(value_weight.shape, BF16),
            pltpu.VMEM((n_t, rows, width), BF16),
            pltpu.VMEM((n_r, rows, width), BF16),
            pltpu.VMEM((n_r, 8, rows), jnp.int32),
            pltpu.VMEM((n_r, rows, 128), F32),
            pltpu.VMEM((n_t, rows, width), BF16),
            pltpu.VMEM((rows, q_w), F32),
            pltpu.VMEM((n_t, per, q_w), BF16),
            pltpu.VMEM((n_t, per, q_w), BF16),
            pltpu.VMEM((n_t, 2, per, k_w), BF16),
            pltpu.VMEM((n_t, 2, per, k_w), BF16),
            pltpu.VMEM((n_r, rank, rows), F32),
            pltpu.VMEM((n_t, n_r, rank, rows), F32),
            pltpu.VMEM((n_r, rows, q_w), F32),
            pltpu.VMEM((n_r, rows, q_w), F32),
            pltpu.SemaphoreType.DMA((3,)),
            sems(n_t), sems(n_r), sems(n_r), sems(n_r), sems(n_t), sems(n_t), sems(n_r), sems(n_t),
        ],
        compiler_params=pltpu.CompilerParams(
            collective_id=0, has_side_effects=True, vmem_limit_bytes=LIMIT
        ),
    )(
        hidden_input,
        norm_gain_vector.reshape(n_t, 1, width),
        ids,
        flat_down(query_down_weight),
        flat_up(query_up_weight),
        query_weight,
        key_weight,
        value_weight,
    )
    q_rows = q_in.transpose(1, 0, 2).reshape(per, n_t * q_w)
    k_rows = kv_in[:, 0].transpose(1, 0, 2).reshape(per, n_t * k_w)
    v_rows = kv_in[:, 1].transpose(1, 0, 2).reshape(per, n_t * k_w)
    context_vectors = attend(q_rows, k_rows, v_rows, key_cache_rows, value_cache_rows, cache_length)
    return pl.pallas_call(
        functools.partial(output_kernel, n_r, n_t, held, rank),
        out_shape=jax.ShapeDtypeStruct((rows, width), BF16),
        in_specs=[VM] * 5 + [ANY],
        out_specs=VM,
        scratch_shapes=[
            pltpu.VMEM(output_weight.shape, BF16),
            pltpu.VMEM((n_t, per, o_w), BF16),
            pltpu.VMEM((n_r, rows, o_w), BF16),
            pltpu.VMEM((n_t, rows, width), F32),
            pltpu.VMEM((n_t, rows, width), F32),
            pltpu.VMEM((n_r, rank, rows), F32),
            pltpu.VMEM((n_t, n_r, rank, rows), F32),
            pltpu.VMEM((n_r, rows, width), F32),
            pltpu.VMEM((n_r, rows, width), F32),
            pltpu.SemaphoreType.DMA((1,)),
            sems(n_t), sems(n_r), sems(n_t), sems(n_t), sems(n_r),
        ],
        compiler_params=pltpu.CompilerParams(
            collective_id=1, has_side_effects=True, vmem_limit_bytes=LIMIT
        ),
    )(
        context_vectors.reshape(per, n_t, o_w).transpose(1, 0, 2),
        hidden_input,
        ids_z,
        flat_down(output_down_weight),
        flat_up(output_up_weight),
        output_weight,
    )


def solution(mesh):
    placed = (
        P(("groups", "replica"), "tensor"),
        P(),
        P(None, "tensor"),
        P(None, "tensor"),
        P(None, "tensor"),
        P("tensor", None),
        P(("groups", "replica", "tensor"), None, None),
        P(("groups", "replica", "tensor"), None, None),
        P(("groups", "replica", "tensor")),
        P(("groups", "replica")),
        P(("groups", "replica"), "tensor", None),
        P(("groups", "replica"), None, "tensor"),
        P(("groups", "replica"), "tensor", None),
        P(("groups", "replica"), None, "tensor"),
    )
    return jax.shard_map(
        functools.partial(per_device, mesh.shape["replica"], mesh.shape["tensor"]),
        mesh=mesh,
        in_specs=placed,
        out_specs=P(("groups", "replica"), "tensor"),
        check_vma=False,
    )
```

```python
import functools

import jax
import jax.numpy as jnp
from jax import lax
from jax.experimental import pallas as pl
from jax.experimental.pallas import tpu as pltpu
from jax.sharding import PartitionSpec as P

QUERY_HEADS = 32
KV = 4
HEAD_SIZE = 128
L = 64


ADAPTER_SCALE = 2.0
ROPE_BASE = 500000.0
EPSILON = 1e-05


def rotate(values, position):
    half = values.shape[-1] // 2
    freq = ROPE_BASE ** (-(jnp.arange(half, dtype=jnp.float32) / half))
    angle = position[:, None, None] * freq[None, None, :]
    first = values[..., :half]
    second = values[..., half:]
    cosine = jnp.cos(angle)
    sine = jnp.sin(angle)
    return jnp.concatenate(
        [first * cosine - second * sine, second * cosine + first * sine], axis=-1
    )


def attend(query_vectors, key_new, value_new, key_cache_rows, value_cache_rows, cache_length):
    count = query_vectors.shape[0]
    group = QUERY_HEADS // KV
    position = cache_length.astype(jnp.float32)
    rot_query = rotate(
        query_vectors.astype(jnp.float32).reshape(count, QUERY_HEADS, HEAD_SIZE), position
    ).astype(jnp.bfloat16)
    rotated_key = rotate(
        key_new.astype(jnp.float32).reshape(count, KV, HEAD_SIZE), position
    ).astype(jnp.bfloat16)
    grouped_query = rot_query.reshape(count, KV, group, HEAD_SIZE)
    keys = key_cache_rows.reshape(count, L, KV, HEAD_SIZE)
    values = value_cache_rows.reshape(count, L, KV, HEAD_SIZE)
    softmax_factor = 1.0 / HEAD_SIZE**0.5
    scores = (
        jnp.einsum("bkgd,blkd->bkgl", grouped_query, keys, preferred_element_type=jnp.float32)
        * softmax_factor
    )
    live = jnp.arange(L)[None, :] < cache_length[:, None]
    scores = jnp.where(live[:, None, None, :], scores, -1e30)
    own_scores = (
        jnp.einsum("enxs,ens->enx", grouped_query, rotated_key, preferred_element_type=jnp.float32)
        * softmax_factor
    )
    top = jnp.maximum(jnp.max(scores, axis=-1), own_scores)
    weights = jnp.exp(scores - top[..., None])
    weight_new = jnp.exp(own_scores - top)
    total = jnp.sum(weights, axis=-1) + weight_new
    probs = (weights / total[..., None]).astype(jnp.bfloat16)
    prob_new = (weight_new / total).astype(jnp.bfloat16)
    context_vectors = jnp.einsum(
        "bkgl,blkd->bkgd", probs, values, preferred_element_type=jnp.float32
    )
    fresh = value_new.reshape(count, KV, 1, HEAD_SIZE).astype(jnp.float32)
    context_vectors = context_vectors + prob_new[..., None].astype(jnp.float32) * fresh
    return context_vectors.astype(jnp.bfloat16).reshape(count, QUERY_HEADS * HEAD_SIZE)


MESH = pl.DeviceIdType.MESH
F32 = jnp.float32
BF16 = jnp.bfloat16


def place():
    group, rep, ten = (lax.axis_index(name) for name in ("groups", "replica", "tensor"))

    def peer_r(step, count):
        other = lax.rem(rep + step, count)
        return other, (group, other, ten)

    def peer_t(step, count):
        other = lax.rem(ten + step, count)
        return other, (group, rep, other)

    return rep, ten, peer_r, peer_t


def meet(n_r, n_t, peer_r, peer_t):
    barrier = pltpu.get_barrier_semaphore()
    for step in range(1, n_t):
        pl.semaphore_signal(barrier, inc=1, device_id=peer_t(step, n_t)[1], device_id_type=MESH)
    for step in range(1, n_r):
        pl.semaphore_signal(barrier, inc=1, device_id=peer_r(step, n_r)[1], device_id_type=MESH)
    pl.semaphore_wait(barrier, n_t + n_r - 2)


def remote(src, dst, sems, step, device):
    copy = pltpu.make_async_remote_copy(
        src_ref=src,
        dst_ref=dst,
        send_sem=sems.at[0, step],
        recv_sem=sems.at[1, step],
        device_id=device,
        device_id_type=MESH,
    )
    copy.start()
    return copy


def held_mask(ids, rep, held, rank):
    shape = (held, rank, ids.shape[1])
    owner = lax.broadcasted_iota(jnp.int32, shape, 0) + rep * held
    return jnp.broadcast_to(ids[0:1, :][None], shape) == owner


def low_of(down, rows, ids, rep, held, rank):
    projected = lax.dot_general(down, rows, (((1,), (1,)), ((), ())), preferred_element_type=F32)
    projected = projected.reshape(held, rank, rows.shape[0])
    return jnp.sum(jnp.where(held_mask(ids, rep, held, rank), projected, 0.0), axis=0)


def up_of(low, up, ids, rep, held, rank):
    low = low.astype(BF16).astype(F32)
    shape = (held, rank, ids.shape[1])
    spread = jnp.where(held_mask(ids, rep, held, rank), jnp.broadcast_to(low[None], shape), 0.0)
    spread = spread.reshape(held * rank, ids.shape[1]).T.astype(BF16)
    return jnp.dot(spread, up, preferred_element_type=F32)


def line_sum(n_r, rep, peer_r, con, arrived, sems_line):
    def hop(side, j, src):
        step = 1 if side == 0 else n_r - 1
        return pltpu.make_async_remote_copy(
            src_ref=src,
            dst_ref=arrived.at[side, j],
            send_sem=sems_line.at[side, 0, j],
            recv_sem=sems_line.at[side, 1, j],
            device_id=peer_r(step, n_r)[1],
            device_id_type=MESH,
        )

    def at_place(i):
        events = [(n_r - 1 - j + i, 0, j) for j in range(i + 1, n_r)]
        events += [(j + n_r - 1 - i, 1, j) for j in range(i)]
        started = []
        for _, side, j in sorted(events):
            first = i == (0 if side == 0 else n_r - 1)
            if not first:
                hop(side, j, arrived.at[side, j]).wait_recv()
                arrived[side, j] = arrived[side, j] + con[j]
            copy = hop(side, j, con.at[j] if first else arrived.at[side, j])
            copy.start()
            started.append(copy)
        for side in range(2):
            if i != (0 if side == 0 else n_r - 1):
                hop(side, i, arrived.at[side, i]).wait_recv()
                con[i] = con[i] + arrived[side, i]
        for copy in started:
            copy.wait_send()

    for i in range(n_r):
        pl.when(rep == i)(functools.partial(at_place, i))


def query_kernel(
    n_r, n_t, held, rank,
    hid, gain, ids, down, up, qw_hbm, kw_hbm, vw_hbm,
    q_out, kv_out, ids_out,
    qw, kw, vw, hid_t, hid_z, ids_z, scale_z, nrm, qbase, qbuf, qin, kvbuf, kvin,
    low_own, low_in, con, con_in,
    wsem, s_hid_t, s_hid_z, s_ids, s_scale, s_kv, s_low, s_con, s_q,
):
    rep, ten, peer_r, peer_t = place()
    rows, width = hid.shape
    loads = [
        pltpu.make_async_copy(src, dst, wsem.at[i])
        for i, (src, dst) in enumerate(((kw_hbm, kw), (vw_hbm, vw), (qw_hbm, qw)))
    ]
    for load in loads:
        load.start()
    meet(n_r, n_t, peer_r, peer_t)
    sent = []
    for step in reversed(range(1, n_t)):
        sent.append(remote(hid, hid_t.at[ten], s_hid_t, step, peer_t(step, n_t)[1]))
    for step in range(1, n_r):
        sent.append(remote(ids, ids_z.at[rep], s_ids, step, peer_r(step, n_r)[1]))
    hidden_z = []
    for step in range(1, n_r):
        hidden_z.append(remote(hid, hid_z.at[rep], s_hid_z, step, peer_r(step, n_r)[1]))
    hid_t[ten] = hid[...]
    ids_z[rep] = ids[...]
    for copy in sent:
        copy.wait()
    total = jnp.zeros((rows, 1), F32)
    for t in range(n_t):
        piece = hid_t[t].astype(F32)
        total = total + jnp.sum(piece * piece, axis=-1, keepdims=True)
    scale = lax.rsqrt(total * (1.0 / (n_t * width)) + EPSILON)
    scale_z[rep] = jnp.broadcast_to(scale, (rows, 128))
    scales = []
    for step in range(1, n_r):
        scales.append(
            remote(scale_z.at[rep], scale_z.at[rep], s_scale, step, peer_r(step, n_r)[1])
        )
    for t in range(n_t):
        nrm[t] = (hid_t[t].astype(F32) * scale * gain[t]).astype(BF16)
    low_own[rep] = low_of(down[...], nrm[ten], ids_z[rep], rep, held, rank)

    def project(weight, t):
        part = weight[pl.ds(pl.multiple_of(t * width, width), width), :]
        return jnp.dot(nrm[t], part, preferred_element_type=F32)

    per = rows // n_t
    for which, (load, weight) in enumerate(((loads[0], kw), (loads[1], vw))):
        load.wait()
        acc = project(weight, 0)
        for t in range(1, n_t):
            acc = acc + project(weight, t)
        kvbuf[:, which] = acc.astype(BF16).reshape(n_t, per, weight.shape[1])
    kvs = []
    for step in range(1, n_t):
        other, device = peer_t(step, n_t)
        kvs.append(remote(kvbuf.at[other], kvin.at[ten], s_kv, step, device))
    kvin[ten] = kvbuf[ten]
    loads[2].wait()
    qbase[...] = project(qw, 0)

    @pl.loop(1, n_t)
    def _(t):
        qbase[...] += project(qw, t)

    for step in range(1, n_r):
        hidden_z[step - 1].wait()
        scales[step - 1].wait()
        source = lax.rem(rep - step + n_r, n_r)
        portion = (hid_z[source].astype(F32) * scale_z[source][:, 0:1] * gain[ten]).astype(BF16)
        low_own[source] = low_of(down[...], portion, ids_z[source], rep, held, rank)
    lows = []
    for step in range(1, n_t):
        lows.append(remote(low_own, low_in.at[ten], s_low, step, peer_t(step, n_t)[1]))
    low_in[ten] = low_own[...]
    for copy in lows:
        copy.wait()
    for other in range(n_r):
        low = low_in[0, other]
        for t in range(1, n_t):
            low = low + low_in[t, other]
        con[other] = up_of(low, up[...], ids_z[other], rep, held, rank)
    line_sum(n_r, rep, peer_r, con, con_in, s_con)
    extra = con[rep]
    query = (qbase[...] + ADAPTER_SCALE * extra).astype(BF16)
    qbuf[...] = query.reshape(qbuf.shape)
    qs = []
    for step in range(1, n_t):
        other, device = peer_t(step, n_t)
        qs.append(remote(qbuf.at[other], qin.at[ten], s_q, step, device))
    qin[ten] = qbuf[ten]
    ids_out[...] = ids_z[...]
    for copy in kvs:
        copy.wait()
    kv_out[...] = kvin[...]
    for copy in qs:
        copy.wait()
    q_out[...] = qin[...]


def output_kernel(
    n_r, n_t, held, rank,
    ctx, hid, ids_z, down, up, ow_hbm,
    out,
    ow, ctx_t, ctx_z, base, base_in, low_own, low_in, con, con_in,
    wsem, s_ctx_t, s_ctx_z, s_base, s_low, s_con,
):
    rep, ten, peer_r, peer_t = place()
    rows, width = hid.shape
    load = pltpu.make_async_copy(ow_hbm, ow, wsem.at[0])
    load.start()
    meet(n_r, n_t, peer_r, peer_t)
    sent = []
    for step in range(1, n_t):
        other, device = peer_t(step, n_t)
        sent.append(remote(ctx.at[other], ctx_t.at[ten], s_ctx_t, step, device))
    ctx_t[ten] = ctx[ten]
    for copy in sent:
        copy.wait()
    local = ctx_t[...].reshape(rows, ctx.shape[2])
    ctx_z[rep] = local
    zs = []
    for step in range(1, n_r):
        zs.append(remote(ctx_z.at[rep], ctx_z.at[rep], s_ctx_z, step, peer_r(step, n_r)[1]))
    low_own[rep] = low_of(down[...], local, ids_z[rep], rep, held, rank)
    load.wait()
    for step in list(range(1, n_t)) + [0]:
        other, _ = peer_t(step, n_t)
        columns = pl.ds(pl.multiple_of(other * width, width), width)
        base[other] = jnp.dot(ctx_z[rep], ow[:, columns], preferred_element_type=F32)
    base_in[ten] = base[ten]
    for step in range(1, n_r):
        zs[step - 1].wait()
        source = lax.rem(rep - step + n_r, n_r)
        low_own[source] = low_of(down[...], ctx_z[source], ids_z[source], rep, held, rank)
    lows = []
    for step in range(1, n_t):
        lows.append(remote(low_own, low_in.at[ten], s_low, step, peer_t(step, n_t)[1]))
    bases = []
    for step in range(1, n_t):
        other, device = peer_t(step, n_t)
        bases.append(remote(base.at[other], base_in.at[ten], s_base, step, device))
    low_in[ten] = low_own[...]
    for copy in lows:
        copy.wait()
    for other in range(n_r):
        low = low_in[0, other]
        for t in range(1, n_t):
            low = low + low_in[t, other]
        con[other] = up_of(low, up[...], ids_z[other], rep, held, rank)
    line_sum(n_r, rep, peer_r, con, con_in, s_con)
    for copy in bases:
        copy.wait()
    total = base_in[0]
    for t in range(1, n_t):
        total = total + base_in[t]
    total = hid[...].astype(F32) + total
    extra = con[rep]
    out[...] = (total + ADAPTER_SCALE * extra).astype(BF16)


VM = pl.BlockSpec(memory_space=pltpu.VMEM)
ANY = pl.BlockSpec(memory_space=pl.ANY)
LIMIT = 54 * 1024 * 1024


def sems(count):
    return pltpu.SemaphoreType.DMA((2, count))


def per_device(
    n_r,
    n_t,
    hidden_input,
    norm_gain_vector,
    query_weight,
    key_weight,
    value_weight,
    output_weight,
    key_cache_rows,
    value_cache_rows,
    cache_length,
    adapter_index,
    query_down_weight,
    query_up_weight,
    output_down_weight,
    output_up_weight,
):
    rows, width = hidden_input.shape
    held, _, rank = query_down_weight.shape
    per = rows // n_t
    q_w, k_w, o_w = query_weight.shape[1], key_weight.shape[1], output_weight.shape[0]

    def flat_down(table):
        return table.transpose(0, 2, 1).reshape(held * rank, table.shape[1])

    def flat_up(table):
        return table.reshape(held * rank, table.shape[2])

    ids = jnp.broadcast_to(adapter_index[None, :], (8, rows))
    q_in, kv_in, ids_z = pl.pallas_call(
        functools.partial(query_kernel, n_r, n_t, held, rank),
        out_shape=(
            jax.ShapeDtypeStruct((n_t, per, q_w), BF16),
            jax.ShapeDtypeStruct((n_t, 2, per, k_w), BF16),
            jax.ShapeDtypeStruct((n_r, 8, rows), jnp.int32),
        ),
        in_specs=[VM] * 5 + [ANY] * 3,
        out_specs=(VM, VM, VM),
        scratch_shapes=[
            pltpu.VMEM(query_weight.shape, BF16),
            pltpu.VMEM(key_weight.shape, BF16),
            pltpu.VMEM(value_weight.shape, BF16),
            pltpu.VMEM((n_t, rows, width), BF16),
            pltpu.VMEM((n_r, rows, width), BF16),
            pltpu.VMEM((n_r, 8, rows), jnp.int32),
            pltpu.VMEM((n_r, rows, 128), F32),
            pltpu.VMEM((n_t, rows, width), BF16),
            pltpu.VMEM((rows, q_w), F32),
            pltpu.VMEM((n_t, per, q_w), BF16),
            pltpu.VMEM((n_t, per, q_w), BF16),
            pltpu.VMEM((n_t, 2, per, k_w), BF16),
            pltpu.VMEM((n_t, 2, per, k_w), BF16),
            pltpu.VMEM((n_r, rank, rows), F32),
            pltpu.VMEM((n_t, n_r, rank, rows), F32),
            pltpu.VMEM((n_r, rows, q_w), F32),
            pltpu.VMEM((2, n_r, rows, q_w), F32),
            pltpu.SemaphoreType.DMA((3,)),
            sems(n_t), sems(n_r), sems(n_r), sems(n_r), sems(n_t), sems(n_t),
            pltpu.SemaphoreType.DMA((2, 2, n_r)), sems(n_t),
        ],
        compiler_params=pltpu.CompilerParams(
            collective_id=0, has_side_effects=True, vmem_limit_bytes=LIMIT
        ),
    )(
        hidden_input,
        norm_gain_vector.reshape(n_t, 1, width),
        ids,
        flat_down(query_down_weight),
        flat_up(query_up_weight),
        query_weight,
        key_weight,
        value_weight,
    )
    q_rows = q_in.transpose(1, 0, 2).reshape(per, n_t * q_w)
    k_rows = kv_in[:, 0].transpose(1, 0, 2).reshape(per, n_t * k_w)
    v_rows = kv_in[:, 1].transpose(1, 0, 2).reshape(per, n_t * k_w)
    context_vectors = attend(q_rows, k_rows, v_rows, key_cache_rows, value_cache_rows, cache_length)
    return pl.pallas_call(
        functools.partial(output_kernel, n_r, n_t, held, rank),
        out_shape=jax.ShapeDtypeStruct((rows, width), BF16),
        in_specs=[VM] * 5 + [ANY],
        out_specs=VM,
        scratch_shapes=[
            pltpu.VMEM(output_weight.shape, BF16),
            pltpu.VMEM((n_t, per, o_w), BF16),
            pltpu.VMEM((n_r, rows, o_w), BF16),
            pltpu.VMEM((n_t, rows, width), F32),
            pltpu.VMEM((n_t, rows, width), F32),
            pltpu.VMEM((n_r, rank, rows), F32),
            pltpu.VMEM((n_t, n_r, rank, rows), F32),
            pltpu.VMEM((n_r, rows, width), F32),
            pltpu.VMEM((2, n_r, rows, width), F32),
            pltpu.SemaphoreType.DMA((1,)),
            sems(n_t), sems(n_r), sems(n_t), sems(n_t),
            pltpu.SemaphoreType.DMA((2, 2, n_r)),
        ],
        compiler_params=pltpu.CompilerParams(
            collective_id=1, has_side_effects=True, vmem_limit_bytes=LIMIT
        ),
    )(
        context_vectors.reshape(per, n_t, o_w).transpose(1, 0, 2),
        hidden_input,
        ids_z,
        flat_down(output_down_weight),
        flat_up(output_up_weight),
        output_weight,
    )


def solution(mesh):
    placed = (
        P(("groups", "replica"), "tensor"),
        P(),
        P(None, "tensor"),
        P(None, "tensor"),
        P(None, "tensor"),
        P("tensor", None),
        P(("groups", "replica", "tensor"), None, None),
        P(("groups", "replica", "tensor"), None, None),
        P(("groups", "replica", "tensor")),
        P(("groups", "replica")),
        P(("groups", "replica"), "tensor", None),
        P(("groups", "replica"), None, "tensor"),
        P(("groups", "replica"), "tensor", None),
        P(("groups", "replica"), None, "tensor"),
    )
    return jax.shard_map(
        functools.partial(per_device, mesh.shape["replica"], mesh.shape["tensor"]),
        mesh=mesh,
        in_specs=placed,
        out_specs=P(("groups", "replica"), "tensor"),
        check_vma=False,
    )
```

```python
import functools

import jax
import jax.numpy as jnp
from jax import lax
from jax.experimental import pallas as pl
from jax.experimental.pallas import tpu as pltpu
from jax.sharding import PartitionSpec as P

QUERY_HEADS = 32
KV = 4
HEAD_SIZE = 128
L = 64


ADAPTER_SCALE = 2.0
ROPE_BASE = 500000.0
EPSILON = 1e-05


def rotate(values, position):
    half = values.shape[-1] // 2
    freq = ROPE_BASE ** (-(jnp.arange(half, dtype=jnp.float32) / half))
    angle = position[:, None, None] * freq[None, None, :]
    first = values[..., :half]
    second = values[..., half:]
    cosine = jnp.cos(angle)
    sine = jnp.sin(angle)
    return jnp.concatenate(
        [first * cosine - second * sine, second * cosine + first * sine], axis=-1
    )


def attend(query_vectors, key_new, value_new, key_cache_rows, value_cache_rows, cache_length):
    count = query_vectors.shape[0]
    group = QUERY_HEADS // KV
    position = cache_length.astype(jnp.float32)
    rot_query = rotate(
        query_vectors.astype(jnp.float32).reshape(count, QUERY_HEADS, HEAD_SIZE), position
    ).astype(jnp.bfloat16)
    rotated_key = rotate(
        key_new.astype(jnp.float32).reshape(count, KV, HEAD_SIZE), position
    ).astype(jnp.bfloat16)
    grouped_query = rot_query.reshape(count, KV, group, HEAD_SIZE)
    keys = key_cache_rows.reshape(count, L, KV, HEAD_SIZE)
    values = value_cache_rows.reshape(count, L, KV, HEAD_SIZE)
    softmax_factor = 1.0 / HEAD_SIZE**0.5
    scores = (
        jnp.einsum("bkgd,blkd->bkgl", grouped_query, keys, preferred_element_type=jnp.float32)
        * softmax_factor
    )
    live = jnp.arange(L)[None, :] < cache_length[:, None]
    scores = jnp.where(live[:, None, None, :], scores, -1e30)
    own_scores = (
        jnp.einsum("enxs,ens->enx", grouped_query, rotated_key, preferred_element_type=jnp.float32)
        * softmax_factor
    )
    top = jnp.maximum(jnp.max(scores, axis=-1), own_scores)
    weights = jnp.exp(scores - top[..., None])
    weight_new = jnp.exp(own_scores - top)
    total = jnp.sum(weights, axis=-1) + weight_new
    probs = (weights / total[..., None]).astype(jnp.bfloat16)
    prob_new = (weight_new / total).astype(jnp.bfloat16)
    context_vectors = jnp.einsum(
        "bkgl,blkd->bkgd", probs, values, preferred_element_type=jnp.float32
    )
    fresh = value_new.reshape(count, KV, 1, HEAD_SIZE).astype(jnp.float32)
    context_vectors = context_vectors + prob_new[..., None].astype(jnp.float32) * fresh
    return context_vectors.astype(jnp.bfloat16).reshape(count, QUERY_HEADS * HEAD_SIZE)


MESH = pl.DeviceIdType.MESH
F32 = jnp.float32
BF16 = jnp.bfloat16


def place():
    group, rep, ten = (lax.axis_index(name) for name in ("groups", "replica", "tensor"))

    def peer_r(step, count):
        other = lax.rem(rep + step, count)
        return other, (group, other, ten)

    def peer_t(step, count):
        other = lax.rem(ten + step, count)
        return other, (group, rep, other)

    return rep, ten, peer_r, peer_t


def meet(n_r, n_t, peer_r, peer_t):
    barrier = pltpu.get_barrier_semaphore()
    for step in range(1, n_t):
        pl.semaphore_signal(barrier, inc=1, device_id=peer_t(step, n_t)[1], device_id_type=MESH)
    for step in range(1, n_r):
        pl.semaphore_signal(barrier, inc=1, device_id=peer_r(step, n_r)[1], device_id_type=MESH)
    pl.semaphore_wait(barrier, n_t + n_r - 2)


def remote(src, dst, sems, step, device):
    copy = pltpu.make_async_remote_copy(
        src_ref=src,
        dst_ref=dst,
        send_sem=sems.at[0, step],
        recv_sem=sems.at[1, step],
        device_id=device,
        device_id_type=MESH,
    )
    copy.start()
    return copy


def held_mask(ids, rep, held, rank):
    shape = (held, rank, ids.shape[1])
    owner = lax.broadcasted_iota(jnp.int32, shape, 0) + rep * held
    return jnp.broadcast_to(ids[0:1, :][None], shape) == owner


def low_of(down, rows, ids, rep, held, rank):
    projected = lax.dot_general(down, rows, (((1,), (1,)), ((), ())), preferred_element_type=F32)
    projected = projected.reshape(held, rank, rows.shape[0])
    return jnp.sum(jnp.where(held_mask(ids, rep, held, rank), projected, 0.0), axis=0)


def up_of(low, up, ids, rep, held, rank):
    low = low.astype(BF16).astype(F32)
    shape = (held, rank, ids.shape[1])
    spread = jnp.where(held_mask(ids, rep, held, rank), jnp.broadcast_to(low[None], shape), 0.0)
    spread = spread.reshape(held * rank, ids.shape[1]).T.astype(BF16)
    return jnp.dot(spread, up, preferred_element_type=F32)


def line_sum(n_r, rep, peer_r, make, con, arrived, sems_line):
    def hop(side, j, src):
        step = 1 if side == 0 else n_r - 1
        return pltpu.make_async_remote_copy(
            src_ref=src,
            dst_ref=arrived.at[side, j],
            send_sem=sems_line.at[side, 0, j],
            recv_sem=sems_line.at[side, 1, j],
            device_id=peer_r(step, n_r)[1],
            device_id_type=MESH,
        )

    def at_place(i):
        events = [(n_r - 1 - j + i, 0, j) for j in range(i + 1, n_r)]
        events += [(j + n_r - 1 - i, 1, j) for j in range(i)]
        started = []
        for _, side, j in sorted(events):
            make(j)
            first = i == (0 if side == 0 else n_r - 1)
            if not first:
                hop(side, j, arrived.at[side, j]).wait_recv()
                arrived[side, j] = arrived[side, j] + con[j]
            copy = hop(side, j, con.at[j] if first else arrived.at[side, j])
            copy.start()
            started.append(copy)
        make(i)
        for side in range(2):
            if i != (0 if side == 0 else n_r - 1):
                hop(side, i, arrived.at[side, i]).wait_recv()
                con[i] = con[i] + arrived[side, i]
        for copy in started:
            copy.wait_send()

    for i in range(n_r):
        pl.when(rep == i)(functools.partial(at_place, i))


def query_kernel(
    n_r, n_t, held, rank,
    hid, gain, ids, down, up, qw_hbm, kw_hbm, vw_hbm,
    q_out, kv_out, ids_out,
    qw, kw, vw, hid_t, hid_z, ids_z, scale_z, nrm, qbase, qbuf, qin, kvbuf, kvin,
    low_own, low_in, con, con_in,
    wsem, s_hid_t, s_hid_z, s_ids, s_scale, s_kv, s_low, s_con, s_q,
):
    rep, ten, peer_r, peer_t = place()
    rows, width = hid.shape
    loads = [
        pltpu.make_async_copy(src, dst, wsem.at[i])
        for i, (src, dst) in enumerate(((kw_hbm, kw), (vw_hbm, vw), (qw_hbm, qw)))
    ]
    for load in loads:
        load.start()
    meet(n_r, n_t, peer_r, peer_t)
    sent = []
    for step in reversed(range(1, n_t)):
        sent.append(remote(hid, hid_t.at[ten], s_hid_t, step, peer_t(step, n_t)[1]))
    for step in range(1, n_r):
        sent.append(remote(ids, ids_z.at[rep], s_ids, step, peer_r(step, n_r)[1]))
    hidden_z = []
    for step in range(1, n_r):
        hidden_z.append(remote(hid, hid_z.at[rep], s_hid_z, step, peer_r(step, n_r)[1]))
    hid_t[ten] = hid[...]
    ids_z[rep] = ids[...]
    for copy in sent:
        copy.wait()
    total = jnp.zeros((rows, 1), F32)
    for t in range(n_t):
        piece = hid_t[t].astype(F32)
        total = total + jnp.sum(piece * piece, axis=-1, keepdims=True)
    scale = lax.rsqrt(total * (1.0 / (n_t * width)) + EPSILON)
    scale_z[rep] = jnp.broadcast_to(scale, (rows, 128))
    scales = []
    for step in range(1, n_r):
        scales.append(
            remote(scale_z.at[rep], scale_z.at[rep], s_scale, step, peer_r(step, n_r)[1])
        )
    for t in range(n_t):
        nrm[t] = (hid_t[t].astype(F32) * scale * gain[t]).astype(BF16)
    low_own[rep] = low_of(down[...], nrm[ten], ids_z[rep], rep, held, rank)

    def project(weight, t):
        part = weight[pl.ds(pl.multiple_of(t * width, width), width), :]
        return jnp.dot(nrm[t], part, preferred_element_type=F32)

    per = rows // n_t
    for which, (load, weight) in enumerate(((loads[0], kw), (loads[1], vw))):
        load.wait()
        acc = project(weight, 0)
        for t in range(1, n_t):
            acc = acc + project(weight, t)
        kvbuf[:, which] = acc.astype(BF16).reshape(n_t, per, weight.shape[1])
    kvs = []
    for step in range(1, n_t):
        other, device = peer_t(step, n_t)
        kvs.append(remote(kvbuf.at[other], kvin.at[ten], s_kv, step, device))
    kvin[ten] = kvbuf[ten]
    loads[2].wait()
    qbase[...] = project(qw, 0)

    @pl.loop(1, n_t)
    def _(t):
        qbase[...] += project(qw, t)

    for step in range(1, n_r):
        hidden_z[step - 1].wait()
        scales[step - 1].wait()
        source = lax.rem(rep - step + n_r, n_r)
        portion = (hid_z[source].astype(F32) * scale_z[source][:, 0:1] * gain[ten]).astype(BF16)
        low_own[source] = low_of(down[...], portion, ids_z[source], rep, held, rank)
    lows = []
    for step in range(1, n_t):
        lows.append(remote(low_own, low_in.at[ten], s_low, step, peer_t(step, n_t)[1]))
    low_in[ten] = low_own[...]
    for copy in lows:
        copy.wait()
    def make(other):
        low = low_in[0, other]
        for t in range(1, n_t):
            low = low + low_in[t, other]
        con[other] = up_of(low, up[...], ids_z[other], rep, held, rank)

    line_sum(n_r, rep, peer_r, make, con, con_in, s_con)
    extra = con[rep]
    query = (qbase[...] + ADAPTER_SCALE * extra).astype(BF16)
    qbuf[...] = query.reshape(qbuf.shape)
    qs = []
    for step in range(1, n_t):
        other, device = peer_t(step, n_t)
        qs.append(remote(qbuf.at[other], qin.at[ten], s_q, step, device))
    qin[ten] = qbuf[ten]
    ids_out[...] = ids_z[...]
    for copy in kvs:
        copy.wait()
    kv_out[...] = kvin[...]
    for copy in qs:
        copy.wait()
    q_out[...] = qin[...]


def output_kernel(
    n_r, n_t, held, rank,
    ctx, hid, ids_z, down, up, ow_hbm,
    out,
    ow, ctx_t, ctx_z, base, base_in, low_own, low_in, con, con_in,
    wsem, s_ctx_t, s_ctx_z, s_base, s_low, s_con,
):
    rep, ten, peer_r, peer_t = place()
    rows, width = hid.shape
    load = pltpu.make_async_copy(ow_hbm, ow, wsem.at[0])
    load.start()
    meet(n_r, n_t, peer_r, peer_t)
    sent = []
    for step in range(1, n_t):
        other, device = peer_t(step, n_t)
        sent.append(remote(ctx.at[other], ctx_t.at[ten], s_ctx_t, step, device))
    ctx_t[ten] = ctx[ten]
    for copy in sent:
        copy.wait()
    local = ctx_t[...].reshape(rows, ctx.shape[2])
    ctx_z[rep] = local
    zs = []
    for step in range(1, n_r):
        zs.append(remote(ctx_z.at[rep], ctx_z.at[rep], s_ctx_z, step, peer_r(step, n_r)[1]))
    low_own[rep] = low_of(down[...], local, ids_z[rep], rep, held, rank)
    load.wait()
    for step in list(range(1, n_t)) + [0]:
        other, _ = peer_t(step, n_t)
        columns = pl.ds(pl.multiple_of(other * width, width), width)
        base[other] = jnp.dot(ctx_z[rep], ow[:, columns], preferred_element_type=F32)
    base_in[ten] = base[ten]
    for step in range(1, n_r):
        zs[step - 1].wait()
        source = lax.rem(rep - step + n_r, n_r)
        low_own[source] = low_of(down[...], ctx_z[source], ids_z[source], rep, held, rank)
    lows = []
    for step in range(1, n_t):
        lows.append(remote(low_own, low_in.at[ten], s_low, step, peer_t(step, n_t)[1]))
    bases = []
    for step in range(1, n_t):
        other, device = peer_t(step, n_t)
        bases.append(remote(base.at[other], base_in.at[ten], s_base, step, device))
    low_in[ten] = low_own[...]
    for copy in lows:
        copy.wait()
    def make(other):
        low = low_in[0, other]
        for t in range(1, n_t):
            low = low + low_in[t, other]
        con[other] = up_of(low, up[...], ids_z[other], rep, held, rank)

    line_sum(n_r, rep, peer_r, make, con, con_in, s_con)
    for copy in bases:
        copy.wait()
    total = base_in[0]
    for t in range(1, n_t):
        total = total + base_in[t]
    total = hid[...].astype(F32) + total
    extra = con[rep]
    out[...] = (total + ADAPTER_SCALE * extra).astype(BF16)


VM = pl.BlockSpec(memory_space=pltpu.VMEM)
ANY = pl.BlockSpec(memory_space=pl.ANY)
LIMIT = 54 * 1024 * 1024


def sems(count):
    return pltpu.SemaphoreType.DMA((2, count))


def per_device(
    n_r,
    n_t,
    hidden_input,
    norm_gain_vector,
    query_weight,
    key_weight,
    value_weight,
    output_weight,
    key_cache_rows,
    value_cache_rows,
    cache_length,
    adapter_index,
    query_down_weight,
    query_up_weight,
    output_down_weight,
    output_up_weight,
):
    rows, width = hidden_input.shape
    held, _, rank = query_down_weight.shape
    per = rows // n_t
    q_w, k_w, o_w = query_weight.shape[1], key_weight.shape[1], output_weight.shape[0]

    def flat_down(table):
        return table.transpose(0, 2, 1).reshape(held * rank, table.shape[1])

    def flat_up(table):
        return table.reshape(held * rank, table.shape[2])

    ids = jnp.broadcast_to(adapter_index[None, :], (8, rows))
    q_in, kv_in, ids_z = pl.pallas_call(
        functools.partial(query_kernel, n_r, n_t, held, rank),
        out_shape=(
            jax.ShapeDtypeStruct((n_t, per, q_w), BF16),
            jax.ShapeDtypeStruct((n_t, 2, per, k_w), BF16),
            jax.ShapeDtypeStruct((n_r, 8, rows), jnp.int32),
        ),
        in_specs=[VM] * 5 + [ANY] * 3,
        out_specs=(VM, VM, VM),
        scratch_shapes=[
            pltpu.VMEM(query_weight.shape, BF16),
            pltpu.VMEM(key_weight.shape, BF16),
            pltpu.VMEM(value_weight.shape, BF16),
            pltpu.VMEM((n_t, rows, width), BF16),
            pltpu.VMEM((n_r, rows, width), BF16),
            pltpu.VMEM((n_r, 8, rows), jnp.int32),
            pltpu.VMEM((n_r, rows, 128), F32),
            pltpu.VMEM((n_t, rows, width), BF16),
            pltpu.VMEM((rows, q_w), F32),
            pltpu.VMEM((n_t, per, q_w), BF16),
            pltpu.VMEM((n_t, per, q_w), BF16),
            pltpu.VMEM((n_t, 2, per, k_w), BF16),
            pltpu.VMEM((n_t, 2, per, k_w), BF16),
            pltpu.VMEM((n_r, rank, rows), F32),
            pltpu.VMEM((n_t, n_r, rank, rows), F32),
            pltpu.VMEM((n_r, rows, q_w), F32),
            pltpu.VMEM((2, n_r, rows, q_w), F32),
            pltpu.SemaphoreType.DMA((3,)),
            sems(n_t), sems(n_r), sems(n_r), sems(n_r), sems(n_t), sems(n_t),
            pltpu.SemaphoreType.DMA((2, 2, n_r)), sems(n_t),
        ],
        compiler_params=pltpu.CompilerParams(
            collective_id=0, has_side_effects=True, vmem_limit_bytes=LIMIT
        ),
    )(
        hidden_input,
        norm_gain_vector.reshape(n_t, 1, width),
        ids,
        flat_down(query_down_weight),
        flat_up(query_up_weight),
        query_weight,
        key_weight,
        value_weight,
    )
    q_rows = q_in.transpose(1, 0, 2).reshape(per, n_t * q_w)
    k_rows = kv_in[:, 0].transpose(1, 0, 2).reshape(per, n_t * k_w)
    v_rows = kv_in[:, 1].transpose(1, 0, 2).reshape(per, n_t * k_w)
    context_vectors = attend(q_rows, k_rows, v_rows, key_cache_rows, value_cache_rows, cache_length)
    return pl.pallas_call(
        functools.partial(output_kernel, n_r, n_t, held, rank),
        out_shape=jax.ShapeDtypeStruct((rows, width), BF16),
        in_specs=[VM] * 5 + [ANY],
        out_specs=VM,
        scratch_shapes=[
            pltpu.VMEM(output_weight.shape, BF16),
            pltpu.VMEM((n_t, per, o_w), BF16),
            pltpu.VMEM((n_r, rows, o_w), BF16),
            pltpu.VMEM((n_t, rows, width), F32),
            pltpu.VMEM((n_t, rows, width), F32),
            pltpu.VMEM((n_r, rank, rows), F32),
            pltpu.VMEM((n_t, n_r, rank, rows), F32),
            pltpu.VMEM((n_r, rows, width), F32),
            pltpu.VMEM((2, n_r, rows, width), F32),
            pltpu.SemaphoreType.DMA((1,)),
            sems(n_t), sems(n_r), sems(n_t), sems(n_t),
            pltpu.SemaphoreType.DMA((2, 2, n_r)),
        ],
        compiler_params=pltpu.CompilerParams(
            collective_id=1, has_side_effects=True, vmem_limit_bytes=LIMIT
        ),
    )(
        context_vectors.reshape(per, n_t, o_w).transpose(1, 0, 2),
        hidden_input,
        ids_z,
        flat_down(output_down_weight),
        flat_up(output_up_weight),
        output_weight,
    )


def solution(mesh):
    placed = (
        P(("groups", "replica"), "tensor"),
        P(),
        P(None, "tensor"),
        P(None, "tensor"),
        P(None, "tensor"),
        P("tensor", None),
        P(("groups", "replica", "tensor"), None, None),
        P(("groups", "replica", "tensor"), None, None),
        P(("groups", "replica", "tensor")),
        P(("groups", "replica")),
        P(("groups", "replica"), "tensor", None),
        P(("groups", "replica"), None, "tensor"),
        P(("groups", "replica"), "tensor", None),
        P(("groups", "replica"), None, "tensor"),
    )
    return jax.shard_map(
        functools.partial(per_device, mesh.shape["replica"], mesh.shape["tensor"]),
        mesh=mesh,
        in_specs=placed,
        out_specs=P(("groups", "replica"), "tensor"),
        check_vma=False,
    )
```

```python
import functools

import jax
import jax.numpy as jnp
from jax import lax
from jax.experimental import pallas as pl
from jax.experimental.pallas import tpu as pltpu
from jax.sharding import PartitionSpec as P

QUERY_HEADS = 32
KV = 4
HEAD_SIZE = 128
L = 64


ADAPTER_SCALE = 2.0
ROPE_BASE = 500000.0
EPSILON = 1e-05


def rotate(values, position):
    half = values.shape[-1] // 2
    freq = ROPE_BASE ** (-(jnp.arange(half, dtype=jnp.float32) / half))
    angle = position[:, None, None] * freq[None, None, :]
    first = values[..., :half]
    second = values[..., half:]
    cosine = jnp.cos(angle)
    sine = jnp.sin(angle)
    return jnp.concatenate(
        [first * cosine - second * sine, second * cosine + first * sine], axis=-1
    )


def attend(query_vectors, key_new, value_new, key_cache_rows, value_cache_rows, cache_length):
    count = query_vectors.shape[0]
    group = QUERY_HEADS // KV
    position = cache_length.astype(jnp.float32)
    rot_query = rotate(
        query_vectors.astype(jnp.float32).reshape(count, QUERY_HEADS, HEAD_SIZE), position
    ).astype(jnp.bfloat16)
    rotated_key = rotate(
        key_new.astype(jnp.float32).reshape(count, KV, HEAD_SIZE), position
    ).astype(jnp.bfloat16)
    grouped_query = rot_query.reshape(count, KV, group, HEAD_SIZE)
    keys = key_cache_rows.reshape(count, L, KV, HEAD_SIZE)
    values = value_cache_rows.reshape(count, L, KV, HEAD_SIZE)
    softmax_factor = 1.0 / HEAD_SIZE**0.5
    scores = (
        jnp.einsum("bkgd,blkd->bkgl", grouped_query, keys, preferred_element_type=jnp.float32)
        * softmax_factor
    )
    live = jnp.arange(L)[None, :] < cache_length[:, None]
    scores = jnp.where(live[:, None, None, :], scores, -1e30)
    own_scores = (
        jnp.einsum("enxs,ens->enx", grouped_query, rotated_key, preferred_element_type=jnp.float32)
        * softmax_factor
    )
    top = jnp.maximum(jnp.max(scores, axis=-1), own_scores)
    weights = jnp.exp(scores - top[..., None])
    weight_new = jnp.exp(own_scores - top)
    total = jnp.sum(weights, axis=-1) + weight_new
    probs = (weights / total[..., None]).astype(jnp.bfloat16)
    prob_new = (weight_new / total).astype(jnp.bfloat16)
    context_vectors = jnp.einsum(
        "bkgl,blkd->bkgd", probs, values, preferred_element_type=jnp.float32
    )
    fresh = value_new.reshape(count, KV, 1, HEAD_SIZE).astype(jnp.float32)
    context_vectors = context_vectors + prob_new[..., None].astype(jnp.float32) * fresh
    return context_vectors.astype(jnp.bfloat16).reshape(count, QUERY_HEADS * HEAD_SIZE)


MESH = pl.DeviceIdType.MESH
F32 = jnp.float32
BF16 = jnp.bfloat16


def place():
    group, rep, ten = (lax.axis_index(name) for name in ("groups", "replica", "tensor"))

    def peer_r(step, count):
        other = lax.rem(rep + step, count)
        return other, (group, other, ten)

    def peer_t(step, count):
        other = lax.rem(ten + step, count)
        return other, (group, rep, other)

    return rep, ten, peer_r, peer_t


def meet(n_r, n_t, peer_r, peer_t):
    barrier = pltpu.get_barrier_semaphore()
    for step in range(1, n_t):
        pl.semaphore_signal(barrier, inc=1, device_id=peer_t(step, n_t)[1], device_id_type=MESH)
    for step in range(1, n_r):
        pl.semaphore_signal(barrier, inc=1, device_id=peer_r(step, n_r)[1], device_id_type=MESH)
    pl.semaphore_wait(barrier, n_t + n_r - 2)


def remote(src, dst, sems, step, device):
    copy = pltpu.make_async_remote_copy(
        src_ref=src,
        dst_ref=dst,
        send_sem=sems.at[0, step],
        recv_sem=sems.at[1, step],
        device_id=device,
        device_id_type=MESH,
    )
    copy.start()
    return copy


def held_mask(ids, rep, held, rank):
    shape = (held, rank, ids.shape[1])
    owner = lax.broadcasted_iota(jnp.int32, shape, 0) + rep * held
    return jnp.broadcast_to(ids[0:1, :][None], shape) == owner


def low_of(down, rows, ids, rep, held, rank):
    projected = lax.dot_general(down, rows, (((1,), (1,)), ((), ())), preferred_element_type=F32)
    projected = projected.reshape(held, rank, rows.shape[0])
    return jnp.sum(jnp.where(held_mask(ids, rep, held, rank), projected, 0.0), axis=0)


def up_of(low, up, ids, rep, held, rank):
    low = low.astype(BF16).astype(F32)
    shape = (held, rank, ids.shape[1])
    spread = jnp.where(held_mask(ids, rep, held, rank), jnp.broadcast_to(low[None], shape), 0.0)
    spread = spread.reshape(held * rank, ids.shape[1]).T.astype(BF16)
    return jnp.dot(spread, up, preferred_element_type=F32)


def line_sum(n_r, rep, peer_r, make, con, arrived, sems_line):
    def hop(side, j, src):
        step = 1 if side == 0 else n_r - 1
        return pltpu.make_async_remote_copy(
            src_ref=src,
            dst_ref=arrived.at[side, j],
            send_sem=sems_line.at[side, 0, j],
            recv_sem=sems_line.at[side, 1, j],
            device_id=peer_r(step, n_r)[1],
            device_id_type=MESH,
        )

    def at_place(i):
        events = [(n_r - 1 - j + i, 0, j) for j in range(i + 1, n_r)]
        events += [(j + n_r - 1 - i, 1, j) for j in range(i)]
        started = []
        for _, side, j in sorted(events):
            make(j)
            first = i == (0 if side == 0 else n_r - 1)
            if not first:
                hop(side, j, arrived.at[side, j]).wait_recv()
                arrived[side, j] = arrived[side, j] + con[j]
            copy = hop(side, j, con.at[j] if first else arrived.at[side, j])
            copy.start()
            started.append(copy)
        make(i)
        for side in range(2):
            if i != (0 if side == 0 else n_r - 1):
                hop(side, i, arrived.at[side, i]).wait_recv()
                con[i] = con[i] + arrived[side, i]
        for copy in started:
            copy.wait_send()

    for i in range(n_r):
        pl.when(rep == i)(functools.partial(at_place, i))


def query_kernel(
    n_r, n_t, held, rank,
    hid, gain, ids, down, up, qw_hbm, kw_hbm, vw_hbm,
    q_out, kv_out, ids_out,
    qw, kw, vw, hid_t, hid_z, ids_z, scale_z, nrm, qbase, qbuf, qin, kvbuf, kvin,
    low_own, low_in, con, con_in,
    wsem, s_hid_t, s_hid_z, s_ids, s_scale, s_kv, s_low, s_con, s_q,
):
    rep, ten, peer_r, peer_t = place()
    rows, width = hid.shape
    loads = [
        pltpu.make_async_copy(src, dst, wsem.at[i])
        for i, (src, dst) in enumerate(((kw_hbm, kw), (vw_hbm, vw), (qw_hbm, qw)))
    ]
    for load in loads:
        load.start()
    meet(n_r, n_t, peer_r, peer_t)
    hidden_z = []
    for step in range(1, n_r):
        hidden_z.append(remote(hid, hid_z.at[rep], s_hid_z, step, peer_r(step, n_r)[1]))
    sent = []
    for step in reversed(range(1, n_t)):
        sent.append(remote(hid, hid_t.at[ten], s_hid_t, step, peer_t(step, n_t)[1]))
    for step in range(1, n_r):
        sent.append(remote(ids, ids_z.at[rep], s_ids, step, peer_r(step, n_r)[1]))
    hid_t[ten] = hid[...]
    ids_z[rep] = ids[...]
    for copy in sent:
        copy.wait()
    total = jnp.zeros((rows, 1), F32)
    for t in range(n_t):
        piece = hid_t[t].astype(F32)
        total = total + jnp.sum(piece * piece, axis=-1, keepdims=True)
    scale = lax.rsqrt(total * (1.0 / (n_t * width)) + EPSILON)
    scale_z[rep] = jnp.broadcast_to(scale, (rows, 128))
    scales = []
    for step in range(1, n_r):
        scales.append(
            remote(scale_z.at[rep], scale_z.at[rep], s_scale, step, peer_r(step, n_r)[1])
        )
    for t in range(n_t):
        nrm[t] = (hid_t[t].astype(F32) * scale * gain[t]).astype(BF16)
    low_own[rep] = low_of(down[...], nrm[ten], ids_z[rep], rep, held, rank)

    def project(weight, t):
        part = weight[pl.ds(pl.multiple_of(t * width, width), width), :]
        return jnp.dot(nrm[t], part, preferred_element_type=F32)

    per = rows // n_t
    for which, (load, weight) in enumerate(((loads[0], kw), (loads[1], vw))):
        load.wait()
        acc = project(weight, 0)
        for t in range(1, n_t):
            acc = acc + project(weight, t)
        kvbuf[:, which] = acc.astype(BF16).reshape(n_t, per, weight.shape[1])
    kvs = []
    for step in range(1, n_t):
        other, device = peer_t(step, n_t)
        kvs.append(remote(kvbuf.at[other], kvin.at[ten], s_kv, step, device))
    kvin[ten] = kvbuf[ten]
    loads[2].wait()
    qbase[...] = project(qw, 0)

    @pl.loop(1, n_t)
    def _(t):
        qbase[...] += project(qw, t)

    for step in range(1, n_r):
        hidden_z[step - 1].wait()
        scales[step - 1].wait()
        source = lax.rem(rep - step + n_r, n_r)
        portion = (hid_z[source].astype(F32) * scale_z[source][:, 0:1] * gain[ten]).astype(BF16)
        low_own[source] = low_of(down[...], portion, ids_z[source], rep, held, rank)
    lows = []
    for step in range(1, n_t):
        lows.append(remote(low_own, low_in.at[ten], s_low, step, peer_t(step, n_t)[1]))
    low_in[ten] = low_own[...]
    for copy in lows:
        copy.wait()
    def make(other):
        low = low_in[0, other]
        for t in range(1, n_t):
            low = low + low_in[t, other]
        con[other] = up_of(low, up[...], ids_z[other], rep, held, rank)

    line_sum(n_r, rep, peer_r, make, con, con_in, s_con)
    extra = con[rep]
    query = (qbase[...] + ADAPTER_SCALE * extra).astype(BF16)
    qbuf[...] = query.reshape(qbuf.shape)
    qs = []
    for step in range(1, n_t):
        other, device = peer_t(step, n_t)
        qs.append(remote(qbuf.at[other], qin.at[ten], s_q, step, device))
    qin[ten] = qbuf[ten]
    ids_out[...] = ids_z[...]
    for copy in kvs:
        copy.wait()
    kv_out[...] = kvin[...]
    for copy in qs:
        copy.wait()
    q_out[...] = qin[...]


def output_kernel(
    n_r, n_t, held, rank,
    ctx, hid, ids_z, down, up, ow_hbm,
    out,
    ow, ctx_t, ctx_z, base, base_in, low_own, low_in, con, con_in,
    wsem, s_ctx_t, s_ctx_z, s_base, s_low, s_con,
):
    rep, ten, peer_r, peer_t = place()
    rows, width = hid.shape
    load = pltpu.make_async_copy(ow_hbm, ow, wsem.at[0])
    load.start()
    meet(n_r, n_t, peer_r, peer_t)
    sent = []
    for step in range(1, n_t):
        other, device = peer_t(step, n_t)
        sent.append(remote(ctx.at[other], ctx_t.at[ten], s_ctx_t, step, device))
    ctx_t[ten] = ctx[ten]
    for copy in sent:
        copy.wait()
    local = ctx_t[...].reshape(rows, ctx.shape[2])
    ctx_z[rep] = local
    zs = []
    for step in range(1, n_r):
        zs.append(remote(ctx_z.at[rep], ctx_z.at[rep], s_ctx_z, step, peer_r(step, n_r)[1]))
    low_own[rep] = low_of(down[...], local, ids_z[rep], rep, held, rank)
    load.wait()
    for step in list(range(1, n_t)) + [0]:
        other, _ = peer_t(step, n_t)
        columns = pl.ds(pl.multiple_of(other * width, width), width)
        base[other] = jnp.dot(ctx_z[rep], ow[:, columns], preferred_element_type=F32)
    base_in[ten] = base[ten]
    for step in range(1, n_r):
        zs[step - 1].wait()
        source = lax.rem(rep - step + n_r, n_r)
        low_own[source] = low_of(down[...], ctx_z[source], ids_z[source], rep, held, rank)
    lows = []
    for step in range(1, n_t):
        lows.append(remote(low_own, low_in.at[ten], s_low, step, peer_t(step, n_t)[1]))
    bases = []
    for step in range(1, n_t):
        other, device = peer_t(step, n_t)
        bases.append(remote(base.at[other], base_in.at[ten], s_base, step, device))
    low_in[ten] = low_own[...]
    for copy in lows:
        copy.wait()
    def make(other):
        low = low_in[0, other]
        for t in range(1, n_t):
            low = low + low_in[t, other]
        con[other] = up_of(low, up[...], ids_z[other], rep, held, rank)

    line_sum(n_r, rep, peer_r, make, con, con_in, s_con)
    for copy in bases:
        copy.wait()
    total = base_in[0]
    for t in range(1, n_t):
        total = total + base_in[t]
    total = hid[...].astype(F32) + total
    extra = con[rep]
    out[...] = (total + ADAPTER_SCALE * extra).astype(BF16)


VM = pl.BlockSpec(memory_space=pltpu.VMEM)
ANY = pl.BlockSpec(memory_space=pl.ANY)
LIMIT = 54 * 1024 * 1024


def sems(count):
    return pltpu.SemaphoreType.DMA((2, count))


def per_device(
    n_r,
    n_t,
    hidden_input,
    norm_gain_vector,
    query_weight,
    key_weight,
    value_weight,
    output_weight,
    key_cache_rows,
    value_cache_rows,
    cache_length,
    adapter_index,
    query_down_weight,
    query_up_weight,
    output_down_weight,
    output_up_weight,
):
    rows, width = hidden_input.shape
    held, _, rank = query_down_weight.shape
    per = rows // n_t
    q_w, k_w, o_w = query_weight.shape[1], key_weight.shape[1], output_weight.shape[0]

    def flat_down(table):
        return table.transpose(0, 2, 1).reshape(held * rank, table.shape[1])

    def flat_up(table):
        return table.reshape(held * rank, table.shape[2])

    ids = jnp.broadcast_to(adapter_index[None, :], (8, rows))
    q_in, kv_in, ids_z = pl.pallas_call(
        functools.partial(query_kernel, n_r, n_t, held, rank),
        out_shape=(
            jax.ShapeDtypeStruct((n_t, per, q_w), BF16),
            jax.ShapeDtypeStruct((n_t, 2, per, k_w), BF16),
            jax.ShapeDtypeStruct((n_r, 8, rows), jnp.int32),
        ),
        in_specs=[VM] * 5 + [ANY] * 3,
        out_specs=(VM, VM, VM),
        scratch_shapes=[
            pltpu.VMEM(query_weight.shape, BF16),
            pltpu.VMEM(key_weight.shape, BF16),
            pltpu.VMEM(value_weight.shape, BF16),
            pltpu.VMEM((n_t, rows, width), BF16),
            pltpu.VMEM((n_r, rows, width), BF16),
            pltpu.VMEM((n_r, 8, rows), jnp.int32),
            pltpu.VMEM((n_r, rows, 128), F32),
            pltpu.VMEM((n_t, rows, width), BF16),
            pltpu.VMEM((rows, q_w), F32),
            pltpu.VMEM((n_t, per, q_w), BF16),
            pltpu.VMEM((n_t, per, q_w), BF16),
            pltpu.VMEM((n_t, 2, per, k_w), BF16),
            pltpu.VMEM((n_t, 2, per, k_w), BF16),
            pltpu.VMEM((n_r, rank, rows), F32),
            pltpu.VMEM((n_t, n_r, rank, rows), F32),
            pltpu.VMEM((n_r, rows, q_w), F32),
            pltpu.VMEM((2, n_r, rows, q_w), F32),
            pltpu.SemaphoreType.DMA((3,)),
            sems(n_t), sems(n_r), sems(n_r), sems(n_r), sems(n_t), sems(n_t),
            pltpu.SemaphoreType.DMA((2, 2, n_r)), sems(n_t),
        ],
        compiler_params=pltpu.CompilerParams(
            collective_id=0, has_side_effects=True, vmem_limit_bytes=LIMIT
        ),
    )(
        hidden_input,
        norm_gain_vector.reshape(n_t, 1, width),
        ids,
        flat_down(query_down_weight),
        flat_up(query_up_weight),
        query_weight,
        key_weight,
        value_weight,
    )
    q_rows = q_in.transpose(1, 0, 2).reshape(per, n_t * q_w)
    k_rows = kv_in[:, 0].transpose(1, 0, 2).reshape(per, n_t * k_w)
    v_rows = kv_in[:, 1].transpose(1, 0, 2).reshape(per, n_t * k_w)
    context_vectors = attend(q_rows, k_rows, v_rows, key_cache_rows, value_cache_rows, cache_length)
    return pl.pallas_call(
        functools.partial(output_kernel, n_r, n_t, held, rank),
        out_shape=jax.ShapeDtypeStruct((rows, width), BF16),
        in_specs=[VM] * 5 + [ANY],
        out_specs=VM,
        scratch_shapes=[
            pltpu.VMEM(output_weight.shape, BF16),
            pltpu.VMEM((n_t, per, o_w), BF16),
            pltpu.VMEM((n_r, rows, o_w), BF16),
            pltpu.VMEM((n_t, rows, width), F32),
            pltpu.VMEM((n_t, rows, width), F32),
            pltpu.VMEM((n_r, rank, rows), F32),
            pltpu.VMEM((n_t, n_r, rank, rows), F32),
            pltpu.VMEM((n_r, rows, width), F32),
            pltpu.VMEM((2, n_r, rows, width), F32),
            pltpu.SemaphoreType.DMA((1,)),
            sems(n_t), sems(n_r), sems(n_t), sems(n_t),
            pltpu.SemaphoreType.DMA((2, 2, n_r)),
        ],
        compiler_params=pltpu.CompilerParams(
            collective_id=1, has_side_effects=True, vmem_limit_bytes=LIMIT
        ),
    )(
        context_vectors.reshape(per, n_t, o_w).transpose(1, 0, 2),
        hidden_input,
        ids_z,
        flat_down(output_down_weight),
        flat_up(output_up_weight),
        output_weight,
    )


def solution(mesh):
    placed = (
        P(("groups", "replica"), "tensor"),
        P(),
        P(None, "tensor"),
        P(None, "tensor"),
        P(None, "tensor"),
        P("tensor", None),
        P(("groups", "replica", "tensor"), None, None),
        P(("groups", "replica", "tensor"), None, None),
        P(("groups", "replica", "tensor")),
        P(("groups", "replica")),
        P(("groups", "replica"), "tensor", None),
        P(("groups", "replica"), None, "tensor"),
        P(("groups", "replica"), "tensor", None),
        P(("groups", "replica"), None, "tensor"),
    )
    return jax.shard_map(
        functools.partial(per_device, mesh.shape["replica"], mesh.shape["tensor"]),
        mesh=mesh,
        in_specs=placed,
        out_specs=P(("groups", "replica"), "tensor"),
        check_vma=False,
    )
```
